256 devices in a mesh: seq: 32 (over z, x), head: 8 (over y, core).
Axes of the slice: x: 4, y: 4, z: 8, core: 2. Of those that a mesh axis runs over, the one named last changes fastest.
Arguments:
- queries: bfloat16 [128, 8192], P('seq', 'head'), may hold values from -15 to 15, as said below
- prefix_keys: bfloat16 [2, 262144, 1024], P(None, 'seq', 'head'), may hold values from -6 to 6, as said below
- prefix_values: bfloat16 [2, 262144, 1024], P(None, 'seq', 'head'), may hold values from -6 to 6
- private_suffix_keys: bfloat16 [128, 1024, 1024], P('seq', None, 'head'), may hold values from -9 to 9
- suffix_values: bfloat16 [128, 1024, 1024], P('seq', None, 'head'), may hold values from -6 to 6
- new_key: bfloat16 [128, 1024], P('seq', 'head'), may hold values from -24 to 24, as said below
- new_value: bfloat16 [128, 1024], P('seq', 'head'), may hold values from -6 to 6
- suffix_lengths: int32 [128], P('seq'), may hold values from 128 to 1024, as said below
- prompt_of: int32 [128], replicated, may hold values from 0 to 1, as said below
- out_weight: bfloat16 [8192, 8192], P('head', 'seq'), may hold values from -0.0625 to 0.0625
Outputs:
- mixed: bfloat16 [128, 8192], P('head', 'seq')
The draws below stay inside these ranges and needn't reach their ends.
Inputs may be any that keep to these rules, and one draw needn't show every extreme that they name: `queries`: every value lies between the bounds. `prefix_keys`: every value lies between the bounds. `new_key`: every value lies between the bounds. `suffix_lengths`: at least 128; some sample uses all 1024 entries. `prompt_of`: each prompt has exactly 64 samples.
All inputs are finite; a program needn't handle non-finite values.
Results may differ from the reference program's by a relative error of at most 0.022.
Values may be sent and summed in bfloat16 or wider, within the bound.
No kernel may reach another device: no remote copies, remote signals or barrier semaphores. Data moves between devices by JAX's collectives and lax.ppermute only.
A program may use at most 128 MiB of HBM per device.

```python
import jax
import jax.numpy as jnp
from jax import lax

D = 8192
HQ = 64
KVH = 8
HEAD_SIZE = 128
PROMPTS = 2
SUF = 1024
PREFIX = 262144
SAMPLES = 128


def base_noise(key):
    return jnp.clip(jax.random.normal(key, (SAMPLES, HQ * HEAD_SIZE), jnp.float32), -5.0, 5.0)


def sign_pattern(key):
    flips = jax.random.bernoulli(jax.random.fold_in(key, 77), 0.5, (HEAD_SIZE,))
    return jnp.where(flips, 1.0, -1.0).astype(jnp.float32)


def draw_queries(key, part):
    noise = base_noise(key)
    pattern = sign_pattern(key)
    key = jax.random.fold_in(key, 1)
    values = 3.0 * noise
    amps = jnp.array([8.0, 9.0, 10.0, 11.0], jnp.float32)[:, None]
    aligned = amps * jnp.tile(pattern, HQ)[None, :]
    values = values.at[:4].set(aligned)
    spread_rows = max(0, min(8, SAMPLES - 4))
    broad = jax.random.uniform(jax.random.fold_in(key, 9), (spread_rows, HQ * HEAD_SIZE), jnp.float32, -15.0, 15.0)
    values = values.at[4:4 + spread_rows].set(broad)
    return values.astype(jnp.bfloat16)


def draw_prefix_keys(key, part):
    pattern = sign_pattern(key)
    key = jax.random.fold_in(key, 2)
    values = jnp.clip(jax.random.normal(key, (PROMPTS, PREFIX, KVH * HEAD_SIZE), jnp.float32), -6.0, 6.0)
    differing = max(1, HEAD_SIZE // 32)
    lowered = jnp.where(jnp.arange(HEAD_SIZE) < differing, 5.0, 5.5).astype(jnp.float32)
    row = jnp.tile(5.5 * pattern, KVH)
    near = jnp.tile(lowered * pattern, KVH)
    values = values.at[:, PREFIX // 3, :].set(row[None, :])
    values = values.at[:, 3 * PREFIX // 4, :].set(near[None, :])
    return values.astype(jnp.bfloat16)


def draw_new_key(key, part):
    noise = base_noise(key)
    key = jax.random.fold_in(key, 3)
    group = HQ // KVH
    weight_of_mean = float(min(group, 4))
    means = jnp.mean(noise.reshape(SAMPLES, KVH, group, HEAD_SIZE), axis=2).reshape(SAMPLES, KVH * HEAD_SIZE)
    extra = jnp.clip(jax.random.normal(key, (SAMPLES, KVH * HEAD_SIZE), jnp.float32), -4.0, 4.0)
    return (weight_of_mean * means + 0.5 * extra).astype(jnp.bfloat16)


def draw_suffix_lengths(key, part):
    key = jax.random.fold_in(key, 4)
    lengths = jax.random.randint(key, (SAMPLES,), SUF // 8, SUF + 1, jnp.int32)
    lengths = lengths.at[0].set(SUF)
    lengths = lengths.at[1].set(SUF // 8)
    return lengths


def draw_prompt_of(key, part):
    key = jax.random.fold_in(key, 5)
    order = jax.random.permutation(key, SAMPLES)
    return (order // (SAMPLES // PROMPTS)).astype(jnp.int32)


def levels(rng, extent, cuts, least, top_value):
    def one(axis_at, shards_of):
        heights = jax.random.uniform(jax.random.fold_in(jax.random.fold_in(rng, 6), axis_at), (shards_of,), jnp.float32, least / len(cuts), top_value / len(cuts))
        return jnp.repeat(jnp.exp(heights), extent[axis_at] // shards_of).reshape((-1,) + (1,) * (len(extent) - axis_at - 1))

    gain = one(*cuts[0])
    for cut in cuts[1:]:
        gain = gain * one(*cut)
    return gain


def scatter_about(key, extent, deviation, most, split=(), kind=jnp.bfloat16):
    loudness = levels(key, extent, split, -0.22, 0.18) if split else 1.0
    values = jax.random.normal(key, extent, jnp.float32) * deviation * loudness
    return jnp.minimum(jnp.maximum(values, -most), most).astype(kind)


def setup_inputs(seed: int = 0) -> dict:
    seeds = jax.random.split(jax.random.key(seed), 11)
    return {
        "queries": draw_queries(jax.random.fold_in(seeds[10], 71), 0),
        "prefix_keys": draw_prefix_keys(jax.random.fold_in(seeds[10], 71), 0),
        "prefix_values": scatter_about(seeds[2], (PROMPTS, PREFIX, KVH * HEAD_SIZE), 1.0, 6.0, ((1, 32), (2, 8))),
        "private_suffix_keys": scatter_about(seeds[3], (SAMPLES, SUF, KVH * HEAD_SIZE), 1.5, 9.0, ((0, 32), (2, 8))),
        "suffix_values": scatter_about(seeds[4], (SAMPLES, SUF, KVH * HEAD_SIZE), 1.0, 6.0, ((0, 32), (2, 8))),
        "new_key": draw_new_key(jax.random.fold_in(seeds[10], 71), 0),
        "new_value": scatter_about(seeds[6], (SAMPLES, KVH * HEAD_SIZE), 1.0, 6.0, ((0, 32), (1, 8))),
        "suffix_lengths": draw_suffix_lengths(jax.random.fold_in(seeds[10], 71), 0),
        "prompt_of": draw_prompt_of(jax.random.fold_in(seeds[10], 71), 0),
        "out_weight": scatter_about(seeds[9], (HQ * HEAD_SIZE, D), (HQ * HEAD_SIZE) ** -0.5, 0.0625, ((0, 8), (1, 32))),
    }


def one_head(qh, kp, vp, key_slice, vs, kn, vn, suffix_length):
    score_scale = 1.0 / (HEAD_SIZE ** 0.5)
    sp = jnp.dot(qh, kp.T, preferred_element_type=jnp.float32) * score_scale
    ss = jnp.dot(qh, key_slice.T, preferred_element_type=jnp.float32) * score_scale
    used = jnp.arange(SUF, dtype=jnp.int32)[None, :] < suffix_length
    ss = jnp.where(used, ss, jnp.float32(-1e30))
    sn = jnp.dot(qh, kn, preferred_element_type=jnp.float32) * score_scale
    top = jnp.maximum(jnp.maximum(jnp.max(sp, axis=-1), jnp.max(ss, axis=-1)), sn)
    ep = jnp.exp(sp - top[:, None])
    es = jnp.exp(ss - top[:, None])
    en = jnp.exp(sn - top)
    total = jnp.sum(ep, axis=-1) + jnp.sum(es, axis=-1) + en
    num = jnp.dot(ep.astype(jnp.bfloat16), vp, preferred_element_type=jnp.float32)
    num = num + jnp.dot(es.astype(jnp.bfloat16), vs, preferred_element_type=jnp.float32)
    num = num + en.astype(jnp.bfloat16).astype(jnp.float32)[:, None] * vn.astype(jnp.float32)[None, :]
    return (num / total[:, None]).astype(jnp.bfloat16)


def reference(queries, prefix_keys, prefix_values, private_suffix_keys, suffix_values, new_key, new_value, suffix_lengths, prompt_of, out_weight):
    group = HQ // KVH

    def per_sample(sample_item):
        query_vector, prompt_index, sample_keys, sample_values, fresh_key, fresh_value, suffix_length = sample_item
        qheads = query_vector.reshape(KVH, group, HEAD_SIZE)

        def per_head(head):
            start_offset = (head * HEAD_SIZE).astype(jnp.int32)
            zero = jnp.int32(0)
            kp = lax.dynamic_slice(prefix_keys, (prompt_index.astype(jnp.int32), zero, start_offset), (1, PREFIX, HEAD_SIZE))[0]
            vp = lax.dynamic_slice(prefix_values, (prompt_index.astype(jnp.int32), zero, start_offset), (1, PREFIX, HEAD_SIZE))[0]
            key_slice = lax.dynamic_slice_in_dim(sample_keys, start_offset, HEAD_SIZE, 1)
            vs = lax.dynamic_slice_in_dim(sample_values, start_offset, HEAD_SIZE, 1)
            kn = lax.dynamic_slice_in_dim(fresh_key, start_offset, HEAD_SIZE, 0)
            vn = lax.dynamic_slice_in_dim(fresh_value, start_offset, HEAD_SIZE, 0)
            qh = lax.dynamic_index_in_dim(qheads, head, 0, keepdims=False)
            return one_head(qh, kp, vp, key_slice, vs, kn, vn, suffix_length)

        heads = lax.map(per_head, jnp.arange(KVH, dtype=jnp.int32))
        return heads.reshape(HQ * HEAD_SIZE)

    context = lax.map(per_sample, (queries, prompt_of, private_suffix_keys, suffix_values, new_key, new_value, suffix_lengths))
    return jnp.dot(context, out_weight, preferred_element_type=jnp.float32).astype(jnp.bfloat16)
```

```python
import functools
import math

import jax
import jax.numpy as jnp
from jax import lax
from jax.experimental import pallas as pl
from jax.experimental.pallas import tpu as pltpu
from jax.sharding import PartitionSpec as P

HEAD_SIZE = 128
NT = (((1,), (1,)), ((), ()))
TN = (((0,), (0,)), ((), ()))


def flash_kernel(sub, prompt_ref, q_ref, k_ref, v_ref, out_ref, qs, acc, top):
    p_at, c_at = pl.program_id(0), pl.program_id(1)
    samples = q_ref.shape[0]
    heads = q_ref.shape[1] // HEAD_SIZE
    per = samples // 2
    rows = per * heads
    scale = 1.0 / HEAD_SIZE**0.5
    c = scale * math.log2(math.e)

    def placing():
        second = (prompt_ref[...] == 1)
        ii = lax.broadcasted_iota(jnp.int32, (samples, samples), 0)
        jj = lax.broadcasted_iota(jnp.int32, (samples, samples), 1)
        upto = (ii <= jj).astype(jnp.bfloat16)
        ones8 = jnp.broadcast_to(second.astype(jnp.float32), (8, samples)).astype(jnp.bfloat16)
        count = jnp.dot(ones8, upto, preferred_element_type=jnp.float32)[:1]
        count = count.astype(jnp.int32)
        at = lax.broadcasted_iota(jnp.int32, (1, samples), 1)
        rank = jnp.where(second, per + count - 1, at - count)
        return (ii == rank).astype(jnp.float32).astype(jnp.bfloat16)

    @pl.when((p_at == 0) & (c_at == 0))
    def _():
        place = placing()
        s = jnp.dot(place, q_ref[...], preferred_element_type=jnp.float32).astype(jnp.bfloat16)
        for p in range(2):
            for h in range(heads):
                qs[p, h*per:(h+1)*per, :] = s[p*per:(p+1)*per, h*HEAD_SIZE:(h+1)*HEAD_SIZE]

    @pl.when(c_at == 0)
    def _():
        top[p_at] = jnp.full(top.shape[1:], -1e30, jnp.float32)
        acc[p_at] = jnp.zeros(acc.shape[1:], jnp.float32)

    q = qs[p_at]
    m = top[p_at]
    a = acc[p_at]
    block = k_ref.shape[1]
    for j in range(block // sub):
        k = k_ref[0, j*sub:(j+1)*sub, :]
        v = v_ref[0, j*sub:(j+1)*sub, :]
        s = lax.dot_general(q, k, NT, preferred_element_type=jnp.float32)
        m_new = jnp.maximum(m, jnp.max(s, axis=1, keepdims=True))
        p = jnp.exp2(s * c - m_new * c).astype(jnp.bfloat16)
        vv = jnp.concatenate([v, jnp.ones_like(v)], axis=1)
        a = a * jnp.exp2((m - m_new) * c) + jnp.dot(p, vv, preferred_element_type=jnp.float32)
        m = m_new
    top[p_at] = m
    acc[p_at] = a

    @pl.when((p_at == 1) & (c_at == pl.num_programs(1) - 1))
    def _():
        place = placing()
        lane = lax.broadcasted_iota(jnp.int32, (per, HEAD_SIZE), 1)
        extra = []
        parts = [[None]*2 for _ in range(heads)]
        for p in range(2):
            mm = top[p] * scale
            m_sent = mm.astype(jnp.bfloat16).astype(jnp.float32)
            aa = acc[p] * jnp.exp(mm - m_sent)
            x = jnp.zeros((per, HEAD_SIZE), jnp.float32)
            for h in range(heads):
                r = slice(h*per, (h+1)*per)
                total = aa[r, HEAD_SIZE:HEAD_SIZE+1]
                hi = total.astype(jnp.bfloat16).astype(jnp.float32)
                x = jnp.where(lane == h, m_sent[r], x)
                x = jnp.where(lane == heads + h, hi, x)
                x = jnp.where(lane == 2*heads + h, total - hi, x)
                parts[h][p] = aa[r, :HEAD_SIZE].astype(jnp.bfloat16)
            extra.append(x.astype(jnp.bfloat16))
        cols = [jnp.concatenate(parts[h], axis=0) for h in range(heads)] + [jnp.concatenate(extra, axis=0)]
        for h, col in enumerate(cols):
            out_ref[:, h*HEAD_SIZE:(h+1)*HEAD_SIZE] = lax.dot_general(place, col, TN, preferred_element_type=jnp.float32).astype(jnp.bfloat16)

def flash(prompt_of, q, k, v, block=8192, sub=1024):
    samples, width = q.shape
    rows = samples // 2 * (width // HEAD_SIZE)
    span = k.shape[1]
    return pl.pallas_call(
        functools.partial(flash_kernel, sub),
        grid=(2, span // block),
        in_specs=[pl.BlockSpec((1, samples), lambda p, c: (0, 0)),
                  pl.BlockSpec((samples, width), lambda p, c: (0, 0)),
                  pl.BlockSpec((1, block, HEAD_SIZE), lambda p, c: (p, c, 0)),
                  pl.BlockSpec((1, block, HEAD_SIZE), lambda p, c: (p, c, 0))],
        out_specs=pl.BlockSpec((samples, width + HEAD_SIZE), lambda p, c: (0, 0)),
        out_shape=jax.ShapeDtypeStruct((samples, width + HEAD_SIZE), jnp.bfloat16),
        scratch_shapes=[pltpu.VMEM((2, rows, HEAD_SIZE), jnp.bfloat16),
                        pltpu.VMEM((2, rows, 2*HEAD_SIZE), jnp.float32),
                        pltpu.VMEM((2, rows, 1), jnp.float32)],
        compiler_params=pltpu.CompilerParams(dimension_semantics=("arbitrary","arbitrary"), vmem_limit_bytes=48*2**20),
        name="prefix",
    )(prompt_of.reshape(1, samples), q, k, v)


def gather(block, axis):
    everyone = jnp.broadcast_to(block[None], (lax.axis_size(axis),) + block.shape)
    return lax.all_to_all(everyone, axis, 0, 0)


def per_device(
    queries,
    prefix_keys,
    prefix_values,
    private_suffix_keys,
    suffix_values,
    new_key,
    new_value,
    suffix_lengths,
    prompt_of,
    out_weight,
):
    score_scale = 1.0 / HEAD_SIZE**0.5
    owned, width = queries.shape
    heads = width // HEAD_SIZE
    capacity = private_suffix_keys.shape[1]
    seq = lax.axis_size("seq")
    f32 = jnp.float32

    every_query = gather(queries, "seq").reshape(seq * owned, width)
    partial = flash(prompt_of, every_query, prefix_keys, prefix_values)
    got = lax.all_to_all(partial.reshape(seq, owned, width + HEAD_SIZE), "seq", 0, 0)

    q = queries.reshape(owned, heads, HEAD_SIZE)
    suffix_scores = (
        jnp.einsum("sgd,std->sgt", q, private_suffix_keys, preferred_element_type=f32) * score_scale
    )
    used = jnp.arange(capacity, dtype=jnp.int32)[None, :] < suffix_lengths[:, None]
    suffix_scores = jnp.where(used[:, None, :], suffix_scores, f32(-1e30))
    new_scores = jnp.einsum("sgd,sd->sg", q, new_key, preferred_element_type=f32) * score_scale
    own_top = jnp.maximum(jnp.max(suffix_scores, axis=-1), new_scores)
    suffix_weights = jnp.exp(suffix_scores - own_top[..., None])
    new_weight = jnp.exp(new_scores - own_top)
    own_total = jnp.sum(suffix_weights, axis=-1) + new_weight
    own_sums = jnp.einsum(
        "sgt,std->sgd",
        suffix_weights.astype(jnp.bfloat16),
        suffix_values,
        preferred_element_type=f32,
    ) + new_weight.astype(jnp.bfloat16).astype(f32)[..., None] * new_value.astype(f32)[:, None, :]

    got = got.astype(f32)
    sums = got[:, :, :width].reshape(seq, owned, heads, HEAD_SIZE)
    tops = got[:, :, width : width + heads]
    totals = (
        got[:, :, width + heads : width + 2 * heads]
        + got[:, :, width + 2 * heads : width + 3 * heads]
    )
    overall = jnp.maximum(jnp.max(tops, axis=0), own_top)
    factors = jnp.exp(tops - overall)
    own_factor = jnp.exp(own_top - overall)
    total = jnp.sum(totals * factors, axis=0) + own_total * own_factor
    numer = jnp.sum(sums * factors[..., None], axis=0) + own_sums * own_factor[..., None]
    context = (numer / total[..., None]).astype(jnp.bfloat16).reshape(owned, width)

    partial_out = jnp.dot(
        gather(context, "seq").reshape(seq * owned, width), out_weight, preferred_element_type=f32
    ).astype(jnp.bfloat16)
    groups = lax.axis_size("head")
    pieces = lax.all_to_all(partial_out.reshape(groups, -1, partial_out.shape[1]), "head", 0, 0)
    return jnp.sum(pieces.astype(f32), axis=0).astype(jnp.bfloat16)


def solution(mesh):
    placed = (
        P("seq", "head"),
        P(None, "seq", "head"),
        P(None, "seq", "head"),
        P("seq", None, "head"),
        P("seq", None, "head"),
        P("seq", "head"),
        P("seq", "head"),
        P("seq"),
        P(),
        P("head", "seq"),
    )
    return jax.shard_map(
        per_device, mesh=mesh, in_specs=placed, out_specs=P("head", "seq"), check_vma=False
    )
```

```python
import math

import jax
import jax.numpy as jnp
from jax import lax
from jax.experimental import pallas as pl
from jax.experimental.pallas import tpu as pltpu
from jax.sharding import PartitionSpec as P

HEAD_SIZE = 128
NT = (((1,), (1,)), ((), ()))
BLOCK = 2048
TILE = 256
PARTS = 2
PREPARE_LIMIT = 4 * 2**20
PREFIX_LIMIT = 40 * 2**20


def prepare_kernel(
    prompt_ref,
    lengths_ref,
    q_ref,
    new_key_ref,
    new_value_ref,
    suffix_keys_hbm,
    suffix_values_hbm,
    keys_hbm,
    keys_ref,
    place_ref,
    back_ref,
    sums_ref,
    tops_ref,
    totals_ref,
    suffix_keys,
    suffix_values,
    sems,
):
    f32 = jnp.float32
    copies = [
        pltpu.make_async_copy(source, target, sems.at[i])
        for i, (source, target) in enumerate(
            (
                (suffix_keys_hbm, suffix_keys),
                (suffix_values_hbm, suffix_values),
                (keys_hbm.at[0], keys_ref),
            )
        )
    ]
    for copy in copies:
        copy.start()

    samples = prompt_ref.shape[1]
    second = prompt_ref[...] == 1
    row = lax.broadcasted_iota(jnp.int32, (samples, samples), 0)
    column = lax.broadcasted_iota(jnp.int32, (samples, samples), 1)
    upto = (row <= column).astype(jnp.bfloat16)
    flags = jnp.broadcast_to(second.astype(f32), (16, samples)).astype(jnp.bfloat16)
    count = jnp.dot(flags, upto, preferred_element_type=f32)[:1].astype(jnp.int32)
    at = lax.broadcasted_iota(jnp.int32, (1, samples), 1)
    rank = jnp.where(second, samples // 2 + count - 1, at - count)
    place = (row == rank).astype(f32)
    place_ref[...] = place.astype(jnp.bfloat16)
    back_ref[...] = place.T.astype(jnp.bfloat16)

    owned, width = q_ref.shape
    heads = width // HEAD_SIZE
    capacity = suffix_keys.shape[1]
    scale = 1.0 / HEAD_SIZE**0.5
    every_q = q_ref[...].astype(f32)
    new_keys = new_key_ref[...].astype(f32)
    new_values = new_value_ref[...].astype(f32)
    position = lax.broadcasted_iota(jnp.int32, (heads, capacity), 1)
    diagonal = lax.broadcasted_iota(jnp.int32, (heads, HEAD_SIZE), 0) == (
        lax.broadcasted_iota(jnp.int32, (heads, HEAD_SIZE), 1)
    )
    copies[0].wait()
    copies[1].wait()
    all_sums, all_tops, all_totals = [], [], []
    for s in range(owned):
        q = jnp.concatenate(
            [every_q[s : s + 1, h * HEAD_SIZE : (h + 1) * HEAD_SIZE] for h in range(heads)], axis=0
        )
        scores = (
            lax.dot_general(
                q.astype(jnp.bfloat16), suffix_keys[s], NT, preferred_element_type=f32
            )
            * scale
        )
        scores = jnp.where(position < lengths_ref[s], scores, -1e30)
        fresh = jnp.sum(q * new_keys[s : s + 1], axis=1, keepdims=True) * scale
        top = jnp.maximum(jnp.max(scores, axis=1, keepdims=True), fresh)
        weights = jnp.exp(scores - top)
        weight = jnp.exp(fresh - top)
        total = jnp.sum(weights, axis=1, keepdims=True) + weight
        sums = (
            jnp.dot(weights.astype(jnp.bfloat16), suffix_values[s], preferred_element_type=f32)
            + weight.astype(jnp.bfloat16).astype(f32) * new_values[s : s + 1]
        )
        all_sums.append(jnp.concatenate([sums[h : h + 1] for h in range(heads)], axis=1))
        all_tops.append(jnp.sum(jnp.where(diagonal, top, 0.0), axis=0, keepdims=True))
        all_totals.append(jnp.sum(jnp.where(diagonal, total, 0.0), axis=0, keepdims=True))
    tops_ref[...] = jnp.concatenate(all_tops, axis=0)
    totals_ref[...] = jnp.concatenate(all_totals, axis=0)
    sums_ref[...] = jnp.concatenate(all_sums, axis=0)
    copies[2].wait()


def prepare(
    prompt_of, lengths, q, new_key, new_value, suffix_keys, suffix_values, prefix_keys
):
    samples = prompt_of.shape[0]
    owned, width = q.shape
    heads = width // HEAD_SIZE
    square = pltpu.VMEM((samples, samples), jnp.bfloat16)
    vmem = pl.BlockSpec(memory_space=pltpu.VMEM)
    hbm = pl.BlockSpec(memory_space=pltpu.HBM)
    lines = jax.ShapeDtypeStruct((owned, HEAD_SIZE), jnp.float32)
    large = [
        pltpu.with_memory_space_constraint(x, pltpu.HBM)
        for x in (suffix_keys, suffix_values, prefix_keys)
    ]
    return pl.pallas_call(
        prepare_kernel,
        in_specs=[vmem, pl.BlockSpec(memory_space=pltpu.SMEM), vmem, vmem, vmem] + [hbm] * 3,
        out_specs=[vmem] * 6,
        out_shape=[
            pltpu.VMEM(prefix_keys.shape[1:], prefix_keys.dtype),
            square,
            square,
            jax.ShapeDtypeStruct((owned, width), jnp.float32),
            lines,
            lines,
        ],
        scratch_shapes=[
            pltpu.VMEM(suffix_keys.shape, suffix_keys.dtype),
            pltpu.VMEM(suffix_values.shape, suffix_values.dtype),
            pltpu.SemaphoreType.DMA((3,)),
        ],
        compiler_params=pltpu.CompilerParams(vmem_limit_bytes=PREPARE_LIMIT),
        cost_estimate=pl.CostEstimate(
            flops=4 * owned * suffix_keys.shape[1] * width,
            bytes_accessed=2 * prefix_keys.size + 4 * suffix_keys.size,
            transcendentals=owned * suffix_keys.shape[1] * heads,
        ),
        name="prepare",
    )(prompt_of.reshape(1, samples), lengths, q, new_key, new_value, *large)


def lane_tops(scores):
    tops = scores[:, :HEAD_SIZE]
    for at in range(HEAD_SIZE, scores.shape[1], HEAD_SIZE):
        tops = jnp.maximum(tops, scores[:, at : at + HEAD_SIZE])
    return tops


def prefix_kernel(
    q_ref,
    place_ref,
    back_ref,
    first_keys,
    keys_hbm,
    values_hbm,
    out_ref,
    second_keys,
    values,
    sorted_q,
    acc,
    top,
    sems,
):
    first_values = pltpu.make_async_copy(values_hbm.at[0], values.at[0], sems.at[0])
    second_copies = [
        pltpu.make_async_copy(keys_hbm.at[1], second_keys, sems.at[1]),
        pltpu.make_async_copy(values_hbm.at[1], values.at[1], sems.at[2]),
    ]
    first_values.start()
    for copy in second_copies:
        copy.start()
    samples, width = q_ref.shape
    heads = width // HEAD_SIZE
    per = samples // 2
    rows = per * heads
    part = rows // PARTS
    span = first_keys.shape[0]
    tiles = BLOCK // TILE
    blocks = span // BLOCK
    f32 = jnp.float32
    scale = math.log2(math.e) / HEAD_SIZE**0.5

    ordered = jnp.dot(place_ref[...], q_ref[...], preferred_element_type=f32) * scale
    for p in range(2):
        for h in range(heads):
            x = ordered[p * per : (p + 1) * per, h * HEAD_SIZE : (h + 1) * HEAD_SIZE]
            high = x.astype(jnp.bfloat16)
            sorted_q[p, h * per : (h + 1) * per, :HEAD_SIZE] = high
            sorted_q[p, h * per : (h + 1) * per, HEAD_SIZE:] = (x - high.astype(f32)).astype(
                jnp.bfloat16
            )

    lane = lax.broadcasted_iota(jnp.int32, (per, HEAD_SIZE), 1)

    def finish(p):
        tops = top[p] * math.log(2.0)
        sent = tops.astype(jnp.bfloat16).astype(f32)
        sums = acc[p] * jnp.exp(tops - sent)
        extra = jnp.zeros((per, HEAD_SIZE), f32)
        pieces = []
        for h in range(heads):
            r = slice(h * per, (h + 1) * per)
            total = sums[r, HEAD_SIZE:]
            high = total.astype(jnp.bfloat16).astype(f32)
            extra = jnp.where(lane == h, sent[r], extra)
            extra = jnp.where(lane == heads + h, high, extra)
            extra = jnp.where(lane == 2 * heads + h, total - high, extra)
            pieces.append(sums[r, :HEAD_SIZE].astype(jnp.bfloat16))
        return jnp.concatenate(pieces + [extra.astype(jnp.bfloat16)], axis=1)

    def score(p, t, r):
        k = (first_keys, second_keys)[p][t * TILE : (t + 1) * TILE, :]
        return lax.dot_general(
            sorted_q[p, r * part : (r + 1) * part],
            jnp.concatenate([k, k], axis=1),
            NT,
            preferred_element_type=f32,
        )

    steps = [(p, j) for p in range(2) for j in range(blocks)]
    scores = [[None] * tiles for _ in range(PARTS)]
    peaks = [None] * PARTS
    for t in range(tiles):
        for r in range(PARTS):
            scores[r][t] = score(0, t, r)
            seen = lane_tops(scores[r][t])
            peaks[r] = seen if t == 0 else jnp.maximum(peaks[r], seen)
    for number, (p, j) in enumerate(steps):
        if j == 0:
            tops = [jnp.full((part, 1), -1e30, f32)] * PARTS
            sums = [jnp.zeros((part, 2 * HEAD_SIZE), f32)] * PARTS
        if number == 0:
            first_values.wait()
        if number == blocks - 1:
            for copy in second_copies:
                copy.wait()
        following = steps[number + 1] if number + 1 < len(steps) else None
        later = [[None] * tiles for _ in range(PARTS)]
        later_peaks = [None] * PARTS
        for r in range(PARTS):
            risen = jnp.maximum(tops[r], jnp.max(peaks[r], axis=1, keepdims=True))
            sums[r] = sums[r] * jnp.exp2(tops[r] - risen)
            tops[r] = risen
        for t in range(tiles):
            for r in range(PARTS):
                if following is not None:
                    later[r][t] = score(following[0], following[1] * tiles + t, r)
                    seen = lane_tops(later[r][t])
                    later_peaks[r] = seen if t == 0 else jnp.maximum(later_peaks[r], seen)
                weights = jnp.exp2(scores[r][t] - tops[r]).astype(jnp.bfloat16)
                first = j * BLOCK + t * TILE
                v = values[p, first : first + TILE, :]
                sums[r] = sums[r] + jnp.dot(
                    weights,
                    jnp.concatenate([v, jnp.ones_like(v)], axis=1),
                    preferred_element_type=f32,
                )
        scores, peaks = later, later_peaks
        if j == blocks - 1:
            for r in range(PARTS):
                top[p, r * part : (r + 1) * part] = tops[r]
                acc[p, r * part : (r + 1) * part] = sums[r]

    both = jnp.concatenate([finish(0), finish(1)], axis=0)
    out_ref[...] = jnp.dot(back_ref[...], both, preferred_element_type=f32).astype(jnp.bfloat16)


def prefix(q, place, back, first_keys, keys, values):
    samples, width = q.shape
    rows = samples // 2 * (width // HEAD_SIZE)
    return pl.pallas_call(
        prefix_kernel,
        in_specs=[pl.BlockSpec(memory_space=pltpu.VMEM)] * 4
        + [pl.BlockSpec(memory_space=pltpu.HBM)] * 2,
        out_specs=pl.BlockSpec(memory_space=pltpu.VMEM),
        out_shape=jax.ShapeDtypeStruct((samples, width + HEAD_SIZE), jnp.bfloat16),
        scratch_shapes=[
            pltpu.VMEM(keys.shape[1:], keys.dtype),
            pltpu.VMEM(values.shape, values.dtype),
            pltpu.VMEM((2, rows, 2 * HEAD_SIZE), jnp.bfloat16),
            pltpu.VMEM((2, rows, 2 * HEAD_SIZE), jnp.float32),
            pltpu.VMEM((2, rows, 1), jnp.float32),
            pltpu.SemaphoreType.DMA((3,)),
        ],
        compiler_params=pltpu.CompilerParams(vmem_limit_bytes=PREFIX_LIMIT),
        name="prefix",
    )(
        q,
        place,
        back,
        pltpu.with_memory_space_constraint(first_keys, pltpu.VMEM),
        pltpu.with_memory_space_constraint(keys, pltpu.HBM),
        pltpu.with_memory_space_constraint(values, pltpu.HBM),
    )


def gather(block, axis):
    everyone = jnp.broadcast_to(block[None], (lax.axis_size(axis),) + block.shape)
    return lax.all_to_all(everyone, axis, 0, 0)


def per_device(
    queries,
    prefix_keys,
    prefix_values,
    private_suffix_keys,
    suffix_values,
    new_key,
    new_value,
    suffix_lengths,
    prompt_of,
    out_weight,
):
    owned, width = queries.shape
    heads = width // HEAD_SIZE
    seq = lax.axis_size("seq")
    f32 = jnp.float32

    first_keys, place, back, own_sums, own_top, own_total = prepare(
        prompt_of,
        suffix_lengths,
        queries,
        new_key,
        new_value,
        private_suffix_keys,
        suffix_values,
        prefix_keys,
    )
    own_sums = own_sums.reshape(owned, heads, HEAD_SIZE)
    own_top = own_top[:, :heads]
    own_total = own_total[:, :heads]
    every_query = gather(queries, "seq").reshape(seq * owned, width)
    partial = prefix(every_query, place, back, first_keys, prefix_keys, prefix_values)
    got = lax.all_to_all(partial.reshape(seq, owned, width + HEAD_SIZE), "seq", 0, 0)

    got = got.astype(f32)
    sums = got[:, :, :width].reshape(seq, owned, heads, HEAD_SIZE)
    tops = got[:, :, width : width + heads]
    totals = (
        got[:, :, width + heads : width + 2 * heads]
        + got[:, :, width + 2 * heads : width + 3 * heads]
    )
    overall = jnp.maximum(jnp.max(tops, axis=0), own_top)
    factors = jnp.exp(tops - overall)
    own_factor = jnp.exp(own_top - overall)
    total = jnp.sum(totals * factors, axis=0) + own_total * own_factor
    numer = jnp.sum(sums * factors[..., None], axis=0) + own_sums * own_factor[..., None]
    context = (numer / total[..., None]).astype(jnp.bfloat16).reshape(owned, width)

    partial_out = jnp.dot(
        gather(context, "seq").reshape(seq * owned, width), out_weight, preferred_element_type=f32
    ).astype(jnp.bfloat16)
    groups = lax.axis_size("head")
    pieces = lax.all_to_all(partial_out.reshape(groups, -1, partial_out.shape[1]), "head", 0, 0)
    return jnp.sum(pieces.astype(f32), axis=0).astype(jnp.bfloat16)


def solution(mesh):
    placed = (
        P("seq", "head"),
        P(None, "seq", "head"),
        P(None, "seq", "head"),
        P("seq", None, "head"),
        P("seq", None, "head"),
        P("seq", "head"),
        P("seq", "head"),
        P("seq"),
        P(),
        P("head", "seq"),
    )
    return jax.shard_map(
        per_device, mesh=mesh, in_specs=placed, out_specs=P("head", "seq"), check_vma=False
    )
```

```python
import math

import jax
import jax.numpy as jnp
from jax import lax
from jax.experimental import pallas as pl
from jax.experimental.pallas import tpu as pltpu
from jax.sharding import PartitionSpec as P

HEAD_SIZE = 128
NT = (((1,), (1,)), ((), ()))
BLOCK = 2048
TILE = 256
PARTS = 2
EARLY = 4096
PREPARE_LIMIT = 4 * 2**20
PREFIX_LIMIT = 40 * 2**20


def prepare_kernel(
    prompt_ref,
    lengths_ref,
    q_ref,
    new_key_ref,
    new_value_ref,
    suffix_keys_hbm,
    suffix_values_hbm,
    keys_hbm,
    values_hbm,
    keys_ref,
    values_ref,
    place_ref,
    back_ref,
    sums_ref,
    tops_ref,
    totals_ref,
    suffix_keys,
    suffix_values,
    sems,
):
    f32 = jnp.float32
    copies = [
        pltpu.make_async_copy(source, target, sems.at[i])
        for i, (source, target) in enumerate(
            (
                (suffix_keys_hbm, suffix_keys),
                (suffix_values_hbm, suffix_values),
                (keys_hbm.at[0, pl.ds(0, keys_ref.shape[0])], keys_ref),
                (values_hbm.at[0, pl.ds(0, values_ref.shape[0])], values_ref),
            )
        )
    ]
    for copy in copies:
        copy.start()

    samples = prompt_ref.shape[1]
    second = prompt_ref[...] == 1
    row = lax.broadcasted_iota(jnp.int32, (samples, samples), 0)
    column = lax.broadcasted_iota(jnp.int32, (samples, samples), 1)
    upto = (row <= column).astype(jnp.bfloat16)
    flags = jnp.broadcast_to(second.astype(f32), (16, samples)).astype(jnp.bfloat16)
    count = jnp.dot(flags, upto, preferred_element_type=f32)[:1].astype(jnp.int32)
    at = lax.broadcasted_iota(jnp.int32, (1, samples), 1)
    rank = jnp.where(second, samples // 2 + count - 1, at - count)
    place = (row == rank).astype(f32)
    place_ref[...] = place.astype(jnp.bfloat16)
    back_ref[...] = place.T.astype(jnp.bfloat16)

    owned, width = q_ref.shape
    heads = width // HEAD_SIZE
    capacity = suffix_keys.shape[1]
    scale = 1.0 / HEAD_SIZE**0.5
    every_q = q_ref[...].astype(f32)
    new_keys = new_key_ref[...].astype(f32)
    new_values = new_value_ref[...].astype(f32)
    position = lax.broadcasted_iota(jnp.int32, (heads, capacity), 1)
    diagonal = lax.broadcasted_iota(jnp.int32, (heads, HEAD_SIZE), 0) == (
        lax.broadcasted_iota(jnp.int32, (heads, HEAD_SIZE), 1)
    )
    copies[0].wait()
    copies[1].wait()
    all_sums, all_tops, all_totals = [], [], []
    for s in range(owned):
        q = jnp.concatenate(
            [every_q[s : s + 1, h * HEAD_SIZE : (h + 1) * HEAD_SIZE] for h in range(heads)], axis=0
        )
        scores = (
            lax.dot_general(
                q.astype(jnp.bfloat16), suffix_keys[s], NT, preferred_element_type=f32
            )
            * scale
        )
        scores = jnp.where(position < lengths_ref[s], scores, -1e30)
        fresh = jnp.sum(q * new_keys[s : s + 1], axis=1, keepdims=True) * scale
        top = jnp.maximum(jnp.max(scores, axis=1, keepdims=True), fresh)
        weights = jnp.exp(scores - top)
        weight = jnp.exp(fresh - top)
        total = jnp.sum(weights, axis=1, keepdims=True) + weight
        sums = (
            jnp.dot(weights.astype(jnp.bfloat16), suffix_values[s], preferred_element_type=f32)
            + weight.astype(jnp.bfloat16).astype(f32) * new_values[s : s + 1]
        )
        all_sums.append(jnp.concatenate([sums[h : h + 1] for h in range(heads)], axis=1))
        all_tops.append(jnp.sum(jnp.where(diagonal, top, 0.0), axis=0, keepdims=True))
        all_totals.append(jnp.sum(jnp.where(diagonal, total, 0.0), axis=0, keepdims=True))
    tops_ref[...] = jnp.concatenate(all_tops, axis=0)
    totals_ref[...] = jnp.concatenate(all_totals, axis=0)
    sums_ref[...] = jnp.concatenate(all_sums, axis=0)
    copies[2].wait()
    copies[3].wait()


def prepare(
    prompt_of, lengths, q, new_key, new_value, suffix_keys, suffix_values, prefix_keys, prefix_values
):
    samples = prompt_of.shape[0]
    owned, width = q.shape
    heads = width // HEAD_SIZE
    square = pltpu.VMEM((samples, samples), jnp.bfloat16)
    vmem = pl.BlockSpec(memory_space=pltpu.VMEM)
    hbm = pl.BlockSpec(memory_space=pltpu.HBM)
    lines = jax.ShapeDtypeStruct((owned, HEAD_SIZE), jnp.float32)
    large = [
        pltpu.with_memory_space_constraint(x, pltpu.HBM)
        for x in (suffix_keys, suffix_values, prefix_keys, prefix_values)
    ]
    return pl.pallas_call(
        prepare_kernel,
        in_specs=[vmem, pl.BlockSpec(memory_space=pltpu.SMEM), vmem, vmem, vmem] + [hbm] * 4,
        out_specs=[vmem] * 7,
        out_shape=[
            pltpu.VMEM((EARLY, HEAD_SIZE), prefix_keys.dtype),
            pltpu.VMEM((EARLY, HEAD_SIZE), prefix_values.dtype),
            square,
            square,
            jax.ShapeDtypeStruct((owned, width), jnp.float32),
            lines,
            lines,
        ],
        scratch_shapes=[
            pltpu.VMEM(suffix_keys.shape, suffix_keys.dtype),
            pltpu.VMEM(suffix_values.shape, suffix_values.dtype),
            pltpu.SemaphoreType.DMA((4,)),
        ],
        compiler_params=pltpu.CompilerParams(vmem_limit_bytes=PREPARE_LIMIT),
        cost_estimate=pl.CostEstimate(
            flops=4 * owned * suffix_keys.shape[1] * width,
            bytes_accessed=4 * EARLY * HEAD_SIZE + 4 * suffix_keys.size,
            transcendentals=owned * suffix_keys.shape[1] * heads,
        ),
        name="prepare",
    )(prompt_of.reshape(1, samples), lengths, q, new_key, new_value, *large)


def lane_tops(scores):
    tops = scores[:, :HEAD_SIZE]
    for at in range(HEAD_SIZE, scores.shape[1], HEAD_SIZE):
        tops = jnp.maximum(tops, scores[:, at : at + HEAD_SIZE])
    return tops


def prefix_kernel(
    q_ref,
    place_ref,
    back_ref,
    early_keys,
    early_values,
    keys_hbm,
    values_hbm,
    out_ref,
    keys,
    values,
    sorted_q,
    acc,
    top,
    sems,
):
    early = early_keys.shape[0]
    span = keys.shape[1]
    rest = pl.ds(early, span - early)
    copies = [
        [
            pltpu.make_async_copy(keys_hbm.at[0, rest], keys.at[0, rest], sems.at[0]),
            pltpu.make_async_copy(values_hbm.at[0, rest], values.at[0, rest], sems.at[1]),
        ],
        [
            pltpu.make_async_copy(keys_hbm.at[1], keys.at[1], sems.at[2]),
            pltpu.make_async_copy(values_hbm.at[1], values.at[1], sems.at[3]),
        ],
    ]
    for copy in copies[0]:
        copy.start()

    def block_of(start, whole, p, first):
        if p == 0 and first < early:
            return start[first : first + TILE, :]
        return whole[p, first : first + TILE, :]

    samples, width = q_ref.shape
    heads = width // HEAD_SIZE
    per = samples // 2
    rows = per * heads
    part = rows // PARTS
    tiles = BLOCK // TILE
    blocks = span // BLOCK
    f32 = jnp.float32
    scale = math.log2(math.e) / HEAD_SIZE**0.5

    ordered = jnp.dot(place_ref[...], q_ref[...], preferred_element_type=f32) * scale
    for p in range(2):
        for h in range(heads):
            x = ordered[p * per : (p + 1) * per, h * HEAD_SIZE : (h + 1) * HEAD_SIZE]
            high = x.astype(jnp.bfloat16)
            sorted_q[p, h * per : (h + 1) * per, :HEAD_SIZE] = high
            sorted_q[p, h * per : (h + 1) * per, HEAD_SIZE:] = (x - high.astype(f32)).astype(
                jnp.bfloat16
            )

    lane = lax.broadcasted_iota(jnp.int32, (per, HEAD_SIZE), 1)

    def finish(p):
        tops = top[p] * math.log(2.0)
        sent = tops.astype(jnp.bfloat16).astype(f32)
        sums = acc[p] * jnp.exp(tops - sent)
        extra = jnp.zeros((per, HEAD_SIZE), f32)
        pieces = []
        for h in range(heads):
            r = slice(h * per, (h + 1) * per)
            total = sums[r, HEAD_SIZE:]
            high = total.astype(jnp.bfloat16).astype(f32)
            extra = jnp.where(lane == h, sent[r], extra)
            extra = jnp.where(lane == heads + h, high, extra)
            extra = jnp.where(lane == 2 * heads + h, total - high, extra)
            pieces.append(sums[r, :HEAD_SIZE].astype(jnp.bfloat16))
        return jnp.concatenate(pieces + [extra.astype(jnp.bfloat16)], axis=1)

    def score(p, t, r):
        k = block_of(early_keys, keys, p, t * TILE)
        return lax.dot_general(
            sorted_q[p, r * part : (r + 1) * part],
            jnp.concatenate([k, k], axis=1),
            NT,
            preferred_element_type=f32,
        )

    finished = []
    steps = [(p, j) for p in range(2) for j in range(blocks)]
    scores = [[None] * tiles for _ in range(PARTS)]
    peaks = [None] * PARTS
    for t in range(tiles):
        for r in range(PARTS):
            scores[r][t] = score(0, t, r)
            seen = lane_tops(scores[r][t])
            peaks[r] = seen if t == 0 else jnp.maximum(peaks[r], seen)
    for number, (p, j) in enumerate(steps):
        if j == 0:
            tops = [jnp.full((part, 1), -1e30, f32)] * PARTS
            sums = [jnp.zeros((part, 2 * HEAD_SIZE), f32)] * PARTS
        if number == 0:
            for copy in copies[1]:
                copy.start()
        if number == early // BLOCK - 1:
            for copy in copies[0]:
                copy.wait()
        if number == blocks - 1:
            for copy in copies[1]:
                copy.wait()
        following = steps[number + 1] if number + 1 < len(steps) else None
        later = [[None] * tiles for _ in range(PARTS)]
        later_peaks = [None] * PARTS
        for r in range(PARTS):
            risen = jnp.maximum(tops[r], jnp.max(peaks[r], axis=1, keepdims=True))
            sums[r] = sums[r] * jnp.exp2(tops[r] - risen)
            tops[r] = risen
        for t in range(tiles):
            for r in range(PARTS):
                if following is not None:
                    later[r][t] = score(following[0], following[1] * tiles + t, r)
                    seen = lane_tops(later[r][t])
                    later_peaks[r] = seen if t == 0 else jnp.maximum(later_peaks[r], seen)
                weights = jnp.exp2(scores[r][t] - tops[r]).astype(jnp.bfloat16)
                first = j * BLOCK + t * TILE
                v = block_of(early_values, values, p, first)
                sums[r] = sums[r] + jnp.dot(
                    weights,
                    jnp.concatenate([v, jnp.ones_like(v)], axis=1),
                    preferred_element_type=f32,
                )
        scores, peaks = later, later_peaks
        if j == blocks - 1:
            for r in range(PARTS):
                top[p, r * part : (r + 1) * part] = tops[r]
                acc[p, r * part : (r + 1) * part] = sums[r]
            finished.append(finish(p))

    both = jnp.concatenate(finished, axis=0)
    out_ref[...] = jnp.dot(back_ref[...], both, preferred_element_type=f32).astype(jnp.bfloat16)


def prefix(q, place, back, early_keys, early_values, keys, values):
    samples, width = q.shape
    rows = samples // 2 * (width // HEAD_SIZE)
    return pl.pallas_call(
        prefix_kernel,
        in_specs=[pl.BlockSpec(memory_space=pltpu.VMEM)] * 5
        + [pl.BlockSpec(memory_space=pltpu.HBM)] * 2,
        out_specs=pl.BlockSpec(memory_space=pltpu.VMEM),
        out_shape=jax.ShapeDtypeStruct((samples, width + HEAD_SIZE), jnp.bfloat16),
        scratch_shapes=[
            pltpu.VMEM(keys.shape, keys.dtype),
            pltpu.VMEM(values.shape, values.dtype),
            pltpu.VMEM((2, rows, 2 * HEAD_SIZE), jnp.bfloat16),
            pltpu.VMEM((2, rows, 2 * HEAD_SIZE), jnp.float32),
            pltpu.VMEM((2, rows, 1), jnp.float32),
            pltpu.SemaphoreType.DMA((4,)),
        ],
        compiler_params=pltpu.CompilerParams(vmem_limit_bytes=PREFIX_LIMIT),
        name="prefix",
    )(
        q,
        place,
        back,
        pltpu.with_memory_space_constraint(early_keys, pltpu.VMEM),
        pltpu.with_memory_space_constraint(early_values, pltpu.VMEM),
        pltpu.with_memory_space_constraint(keys, pltpu.HBM),
        pltpu.with_memory_space_constraint(values, pltpu.HBM),
    )


def gather(block, axis):
    everyone = jnp.broadcast_to(block[None], (lax.axis_size(axis),) + block.shape)
    return lax.all_to_all(everyone, axis, 0, 0)


def per_device(
    queries,
    prefix_keys,
    prefix_values,
    private_suffix_keys,
    suffix_values,
    new_key,
    new_value,
    suffix_lengths,
    prompt_of,
    out_weight,
):
    owned, width = queries.shape
    heads = width // HEAD_SIZE
    seq = lax.axis_size("seq")
    f32 = jnp.float32

    early_keys, early_values, place, back, own_sums, own_top, own_total = prepare(
        prompt_of,
        suffix_lengths,
        queries,
        new_key,
        new_value,
        private_suffix_keys,
        suffix_values,
        prefix_keys,
        prefix_values,
    )
    own_sums = own_sums.reshape(owned, heads, HEAD_SIZE)
    own_top = own_top[:, :heads]
    own_total = own_total[:, :heads]
    every_query = gather(queries, "seq").reshape(seq * owned, width)
    partial = prefix(
        every_query, place, back, early_keys, early_values, prefix_keys, prefix_values
    )
    got = lax.all_to_all(partial.reshape(seq, owned, width + HEAD_SIZE), "seq", 0, 0)

    got = got.astype(f32)
    sums = got[:, :, :width].reshape(seq, owned, heads, HEAD_SIZE)
    tops = got[:, :, width : width + heads]
    totals = (
        got[:, :, width + heads : width + 2 * heads]
        + got[:, :, width + 2 * heads : width + 3 * heads]
    )
    overall = jnp.maximum(jnp.max(tops, axis=0), own_top)
    factors = jnp.exp(tops - overall)
    own_factor = jnp.exp(own_top - overall)
    total = jnp.sum(totals * factors, axis=0) + own_total * own_factor
    numer = jnp.sum(sums * factors[..., None], axis=0) + own_sums * own_factor[..., None]
    context = (numer / total[..., None]).astype(jnp.bfloat16).reshape(owned, width)

    partial_out = jnp.dot(
        gather(context, "seq").reshape(seq * owned, width), out_weight, preferred_element_type=f32
    ).astype(jnp.bfloat16)
    groups = lax.axis_size("head")
    pieces = lax.all_to_all(partial_out.reshape(groups, -1, partial_out.shape[1]), "head", 0, 0)
    return jnp.sum(pieces.astype(f32), axis=0).astype(jnp.bfloat16)


def solution(mesh):
    placed = (
        P("seq", "head"),
        P(None, "seq", "head"),
        P(None, "seq", "head"),
        P("seq", None, "head"),
        P("seq", None, "head"),
        P("seq", "head"),
        P("seq", "head"),
        P("seq"),
        P(),
        P("head", "seq"),
    )
    return jax.shard_map(
        per_device, mesh=mesh, in_specs=placed, out_specs=P("head", "seq"), check_vma=False
    )
```

```python
import math

import jax
import jax.numpy as jnp
from jax import lax
from jax.experimental import pallas as pl
from jax.experimental.pallas import tpu as pltpu
from jax.sharding import PartitionSpec as P

HEAD_SIZE = 128
NT = (((1,), (1,)), ((), ()))
BLOCK = 2048
TILE = 256
PARTS = 2
EARLY = 4096
PREPARE_LIMIT = 4 * 2**20
PREFIX_LIMIT = 40 * 2**20


def prepare_kernel(
    prompt_ref,
    lengths_ref,
    q_ref,
    new_key_ref,
    new_value_ref,
    suffix_keys_hbm,
    suffix_values_hbm,
    keys_hbm,
    values_hbm,
    keys_ref,
    values_ref,
    place_ref,
    back_ref,
    sums_ref,
    tops_ref,
    totals_ref,
    suffix_keys,
    suffix_values,
    sems,
):
    f32 = jnp.float32
    copies = [
        pltpu.make_async_copy(source, target, sems.at[i])
        for i, (source, target) in enumerate(
            (
                (suffix_keys_hbm, suffix_keys),
                (suffix_values_hbm, suffix_values),
                (keys_hbm.at[0, pl.ds(0, keys_ref.shape[0])], keys_ref),
                (values_hbm.at[0, pl.ds(0, values_ref.shape[0])], values_ref),
            )
        )
    ]
    for copy in copies:
        copy.start()

    samples = prompt_ref.shape[1]
    second = prompt_ref[...] == 1
    row = lax.broadcasted_iota(jnp.int32, (samples, samples), 0)
    column = lax.broadcasted_iota(jnp.int32, (samples, samples), 1)
    upto = (row <= column).astype(jnp.bfloat16)
    flags = jnp.broadcast_to(second.astype(f32), (16, samples)).astype(jnp.bfloat16)
    count = jnp.dot(flags, upto, preferred_element_type=f32)[:1].astype(jnp.int32)
    at = lax.broadcasted_iota(jnp.int32, (1, samples), 1)
    rank = jnp.where(second, samples // 2 + count - 1, at - count)
    place = (row == rank).astype(f32)
    place_ref[...] = place.astype(jnp.bfloat16)
    back_ref[...] = place.T.astype(jnp.bfloat16)

    owned, width = q_ref.shape
    heads = width // HEAD_SIZE
    capacity = suffix_keys.shape[1]
    scale = 1.0 / HEAD_SIZE**0.5
    every_q = q_ref[...].astype(f32)
    new_keys = new_key_ref[...].astype(f32)
    new_values = new_value_ref[...].astype(f32)
    position = lax.broadcasted_iota(jnp.int32, (heads, capacity), 1)
    diagonal = lax.broadcasted_iota(jnp.int32, (heads, HEAD_SIZE), 0) == (
        lax.broadcasted_iota(jnp.int32, (heads, HEAD_SIZE), 1)
    )
    copies[0].wait()
    copies[1].wait()
    all_sums, all_tops, all_totals = [], [], []
    for s in range(owned):
        q = jnp.concatenate(
            [every_q[s : s + 1, h * HEAD_SIZE : (h + 1) * HEAD_SIZE] for h in range(heads)], axis=0
        )
        scores = (
            lax.dot_general(
                q.astype(jnp.bfloat16), suffix_keys[s], NT, preferred_element_type=f32
            )
            * scale
        )
        scores = jnp.where(position < lengths_ref[s], scores, -1e30)
        fresh = jnp.sum(q * new_keys[s : s + 1], axis=1, keepdims=True) * scale
        top = jnp.maximum(jnp.max(scores, axis=1, keepdims=True), fresh)
        weights = jnp.exp(scores - top)
        weight = jnp.exp(fresh - top)
        total = jnp.sum(weights, axis=1, keepdims=True) + weight
        sums = (
            jnp.dot(weights.astype(jnp.bfloat16), suffix_values[s], preferred_element_type=f32)
            + weight.astype(jnp.bfloat16).astype(f32) * new_values[s : s + 1]
        )
        all_sums.append(jnp.concatenate([sums[h : h + 1] for h in range(heads)], axis=1))
        all_tops.append(jnp.sum(jnp.where(diagonal, top, 0.0), axis=0, keepdims=True))
        all_totals.append(jnp.sum(jnp.where(diagonal, total, 0.0), axis=0, keepdims=True))
    tops_ref[...] = jnp.concatenate(all_tops, axis=0)
    totals_ref[...] = jnp.concatenate(all_totals, axis=0)
    sums_ref[...] = jnp.concatenate(all_sums, axis=0)
    copies[2].wait()
    copies[3].wait()


def prepare(
    prompt_of, lengths, q, new_key, new_value, suffix_keys, suffix_values, prefix_keys, prefix_values
):
    samples = prompt_of.shape[0]
    owned, width = q.shape
    heads = width // HEAD_SIZE
    square = pltpu.VMEM((samples, samples), jnp.bfloat16)
    vmem = pl.BlockSpec(memory_space=pltpu.VMEM)
    hbm = pl.BlockSpec(memory_space=pltpu.HBM)
    lines = jax.ShapeDtypeStruct((owned, HEAD_SIZE), jnp.float32)
    large = [
        pltpu.with_memory_space_constraint(x, pltpu.HBM)
        for x in (suffix_keys, suffix_values, prefix_keys, prefix_values)
    ]
    return pl.pallas_call(
        prepare_kernel,
        in_specs=[vmem, pl.BlockSpec(memory_space=pltpu.SMEM), vmem, vmem, vmem] + [hbm] * 4,
        out_specs=[vmem] * 7,
        out_shape=[
            pltpu.VMEM((EARLY, HEAD_SIZE), prefix_keys.dtype),
            pltpu.VMEM((EARLY, HEAD_SIZE), prefix_values.dtype),
            square,
            square,
            jax.ShapeDtypeStruct((owned, width), jnp.float32),
            lines,
            lines,
        ],
        scratch_shapes=[
            pltpu.VMEM(suffix_keys.shape, suffix_keys.dtype),
            pltpu.VMEM(suffix_values.shape, suffix_values.dtype),
            pltpu.SemaphoreType.DMA((4,)),
        ],
        compiler_params=pltpu.CompilerParams(vmem_limit_bytes=PREPARE_LIMIT),
        cost_estimate=pl.CostEstimate(
            flops=4 * owned * suffix_keys.shape[1] * width,
            bytes_accessed=4 * EARLY * HEAD_SIZE + 4 * suffix_keys.size,
            transcendentals=owned * suffix_keys.shape[1] * heads,
        ),
        name="prepare",
    )(prompt_of.reshape(1, samples), lengths, q, new_key, new_value, *large)


def lane_tops(scores):
    tops = scores[:, :HEAD_SIZE]
    for at in range(HEAD_SIZE, scores.shape[1], HEAD_SIZE):
        tops = jnp.maximum(tops, scores[:, at : at + HEAD_SIZE])
    return tops


def prefix_kernel(
    q_ref,
    place_ref,
    back_ref,
    early_keys,
    early_values,
    keys_hbm,
    values_hbm,
    out_ref,
    keys,
    values,
    sorted_q,
    acc,
    top,
    sems,
):
    early = early_keys.shape[0]
    span = keys.shape[1]
    rest = pl.ds(early, span - early)
    copies = [
        [
            pltpu.make_async_copy(keys_hbm.at[0, rest], keys.at[0, rest], sems.at[0]),
            pltpu.make_async_copy(values_hbm.at[0, rest], values.at[0, rest], sems.at[1]),
        ],
        [
            pltpu.make_async_copy(keys_hbm.at[1], keys.at[1], sems.at[2]),
            pltpu.make_async_copy(values_hbm.at[1], values.at[1], sems.at[3]),
        ],
    ]
    for copy in copies[0]:
        copy.start()

    def block_of(start, whole, p, first):
        if p == 0 and first < early:
            return start[first : first + TILE, :]
        return whole[p, first : first + TILE, :]

    samples, width = q_ref.shape
    heads = width // HEAD_SIZE
    per = samples // 2
    rows = per * heads
    part = rows // PARTS
    tiles = BLOCK // TILE
    blocks = span // BLOCK
    f32 = jnp.float32
    scale = math.log2(math.e) / HEAD_SIZE**0.5

    ordered = jnp.dot(place_ref[...], q_ref[...], preferred_element_type=f32) * scale
    for p in range(2):
        for h in range(heads):
            x = ordered[p * per : (p + 1) * per, h * HEAD_SIZE : (h + 1) * HEAD_SIZE]
            high = x.astype(jnp.bfloat16)
            sorted_q[p, h * per : (h + 1) * per, :HEAD_SIZE] = high
            sorted_q[p, h * per : (h + 1) * per, HEAD_SIZE:] = (x - high.astype(f32)).astype(
                jnp.bfloat16
            )

    lane = lax.broadcasted_iota(jnp.int32, (per, HEAD_SIZE), 1)

    def finish(p):
        tops = top[p] * math.log(2.0)
        sent = tops.astype(jnp.bfloat16).astype(f32)
        sums = acc[p] * jnp.exp(tops - sent)
        extra = jnp.zeros((per, HEAD_SIZE), f32)
        pieces = []
        for h in range(heads):
            r = slice(h * per, (h + 1) * per)
            total = sums[r, HEAD_SIZE:]
            high = total.astype(jnp.bfloat16).astype(f32)
            extra = jnp.where(lane == h, sent[r], extra)
            extra = jnp.where(lane == heads + h, high, extra)
            extra = jnp.where(lane == 2 * heads + h, total - high, extra)
            pieces.append(sums[r, :HEAD_SIZE].astype(jnp.bfloat16))
        return jnp.concatenate(pieces + [extra.astype(jnp.bfloat16)], axis=1)

    def score(p, t, r):
        k = block_of(early_keys, keys, p, t * TILE)
        return lax.dot_general(
            sorted_q[p, r * part : (r + 1) * part],
            jnp.concatenate([k, k], axis=1),
            NT,
            preferred_element_type=f32,
        )

    finished = []
    steps = [(p, j) for p in range(2) for j in range(blocks)]
    scores = [[None] * tiles for _ in range(PARTS)]
    peaks = [None] * PARTS
    for t in range(tiles):
        for r in range(PARTS):
            scores[r][t] = score(0, t, r)
            seen = lane_tops(scores[r][t])
            peaks[r] = seen if t == 0 else jnp.maximum(peaks[r], seen)
    for number, (p, j) in enumerate(steps):
        if j == 0:
            tops = [jnp.full((part, 1), -1e30, f32)] * PARTS
            sums = [jnp.zeros((part, 2 * HEAD_SIZE), f32)] * PARTS
        if number == 0:
            for copy in copies[1]:
                copy.start()
        if number == early // BLOCK - 1:
            for copy in copies[0]:
                copy.wait()
        if number == blocks - 1:
            for copy in copies[1]:
                copy.wait()
        following = steps[number + 1] if number + 1 < len(steps) else None
        later = [[None] * tiles for _ in range(PARTS)]
        later_peaks = [None] * PARTS
        for r in range(PARTS):
            risen = jnp.maximum(tops[r], jnp.max(peaks[r], axis=1, keepdims=True))
            sums[r] = sums[r] * jnp.exp2(tops[r] - risen)
            tops[r] = risen
        for t in range(tiles):
            for r in range(PARTS):
                if following is not None:
                    later[r][t] = score(following[0], following[1] * tiles + t, r)
                    seen = lane_tops(later[r][t])
                    later_peaks[r] = seen if t == 0 else jnp.maximum(later_peaks[r], seen)
                weights = jnp.exp2(scores[r][t] - tops[r]).astype(jnp.bfloat16)
                first = j * BLOCK + t * TILE
                v = block_of(early_values, values, p, first)
                sums[r] = sums[r] + jnp.dot(
                    weights,
                    jnp.concatenate([v, jnp.ones_like(v)], axis=1),
                    preferred_element_type=f32,
                )
        scores, peaks = later, later_peaks
        if j == blocks - 1:
            for r in range(PARTS):
                top[p, r * part : (r + 1) * part] = tops[r]
                acc[p, r * part : (r + 1) * part] = sums[r]
            finished.append(finish(p))

    both = jnp.concatenate(finished, axis=0)
    out_ref[...] = jnp.dot(back_ref[...], both, preferred_element_type=f32).astype(jnp.bfloat16)


def prefix(q, place, back, early_keys, early_values, keys, values):
    samples, width = q.shape
    rows = samples // 2 * (width // HEAD_SIZE)
    return pl.pallas_call(
        prefix_kernel,
        in_specs=[pl.BlockSpec(memory_space=pltpu.VMEM)] * 5
        + [pl.BlockSpec(memory_space=pltpu.HBM)] * 2,
        out_specs=pl.BlockSpec(memory_space=pltpu.VMEM),
        out_shape=jax.ShapeDtypeStruct((samples, width + HEAD_SIZE), jnp.bfloat16),
        scratch_shapes=[
            pltpu.VMEM(keys.shape, keys.dtype),
            pltpu.VMEM(values.shape, values.dtype),
            pltpu.VMEM((2, rows, 2 * HEAD_SIZE), jnp.bfloat16),
            pltpu.VMEM((2, rows, 2 * HEAD_SIZE), jnp.float32),
            pltpu.VMEM((2, rows, 1), jnp.float32),
            pltpu.SemaphoreType.DMA((4,)),
        ],
        compiler_params=pltpu.CompilerParams(vmem_limit_bytes=PREFIX_LIMIT),
        name="prefix",
    )(
        q,
        place,
        back,
        pltpu.with_memory_space_constraint(early_keys, pltpu.VMEM),
        pltpu.with_memory_space_constraint(early_values, pltpu.VMEM),
        pltpu.with_memory_space_constraint(keys, pltpu.HBM),
        pltpu.with_memory_space_constraint(values, pltpu.HBM),
    )


def gather(block, axis):
    everyone = jnp.broadcast_to(block[None], (lax.axis_size(axis),) + block.shape)
    return lax.all_to_all(everyone, axis, 0, 0)


def per_device(
    queries,
    prefix_keys,
    prefix_values,
    private_suffix_keys,
    suffix_values,
    new_key,
    new_value,
    suffix_lengths,
    prompt_of,
    out_weight,
):
    owned, width = queries.shape
    heads = width // HEAD_SIZE
    seq = lax.axis_size("seq")
    f32 = jnp.float32

    early_keys, early_values, place, back, own_sums, own_top, own_total = prepare(
        prompt_of,
        suffix_lengths,
        queries,
        new_key,
        new_value,
        private_suffix_keys,
        suffix_values,
        prefix_keys,
        prefix_values,
    )
    own_top = own_top[:, :heads]
    own_total = own_total[:, :heads]
    every_query = gather(queries, "seq").reshape(seq * owned, width)
    partial = prefix(
        every_query, place, back, early_keys, early_values, prefix_keys, prefix_values
    )
    got = lax.all_to_all(partial.reshape(seq, owned, width + HEAD_SIZE), "seq", 0, 0)

    got = got.astype(f32)
    tops = got[:, :, width : width + heads]
    totals = (
        got[:, :, width + heads : width + 2 * heads]
        + got[:, :, width + 2 * heads : width + 3 * heads]
    )
    overall = jnp.maximum(jnp.max(tops, axis=0), own_top)
    factors = jnp.exp(tops - overall)
    own_factor = jnp.exp(own_top - overall)
    total = jnp.sum(totals * factors, axis=0) + own_total * own_factor
    pieces = []
    for h in range(heads):
        columns = slice(h * HEAD_SIZE, (h + 1) * HEAD_SIZE)
        numer = jnp.sum(got[:, :, columns] * factors[:, :, h : h + 1], axis=0)
        numer = numer + own_sums[:, columns] * own_factor[:, h : h + 1]
        pieces.append((numer / total[:, h : h + 1]).astype(jnp.bfloat16))
    context = jnp.concatenate(pieces, axis=1)

    partial_out = jnp.dot(
        gather(context, "seq").reshape(seq * owned, width), out_weight, preferred_element_type=f32
    ).astype(jnp.bfloat16)
    groups = lax.axis_size("head")
    pieces = lax.all_to_all(partial_out.reshape(groups, -1, partial_out.shape[1]), "head", 0, 0)
    return jnp.sum(pieces.astype(f32), axis=0).astype(jnp.bfloat16)


def solution(mesh):
    placed = (
        P("seq", "head"),
        P(None, "seq", "head"),
        P(None, "seq", "head"),
        P("seq", None, "head"),
        P("seq", None, "head"),
        P("seq", "head"),
        P("seq", "head"),
        P("seq"),
        P(),
        P("head", "seq"),
    )
    return jax.shard_map(
        per_device, mesh=mesh, in_specs=placed, out_specs=P("head", "seq"), check_vma=False
    )
```
